32 devices in a mesh: expert: 4 (over y, x), tile: 8 (over z, core).
Axes of the slice: x: 2, y: 2, z: 4, core: 2. Of those that a mesh axis runs over, the one named last changes fastest.
Arguments:
- activations: bfloat16 [1536, 6144], P(('expert', 'tile')), may hold values from -40 to 40
- expert_ids: int32 [1536, 2], P(('expert', 'tile')), may hold values from 0 to 3, all different within a row; in each aligned block of 48 rows (0 to 47, 48 to 95, ...) at most 48 rows name the same one
Outputs:
- hessian: float32 [4, 6144, 6144], P('expert', 'tile')
- panels: float32 [4, 6144, 1536], P('expert', 'tile')
The draws below stay inside these ranges and needn't reach their ends.
Inputs may be any that keep to these rules, and one draw needn't show every extreme that they name: `expert_ids`: each row names 2 different experts; within the rows of one device no expert is named more than 48 times, a bound that some block reaches; every expert is named by some row.
All inputs are finite; a program needn't handle non-finite values.
Results may differ from the reference program's by a relative error of at most 0.0003.
Values may be sent and summed in bfloat16 or wider, within the bound.
A program may use at most 256 MiB of HBM per device.

```python
import math
import jax
import jax.numpy as jnp
import numpy as np
from jax import lax

D = 6144
TOP = 2
EXPERTS = 4
TOK_DEV = 48
PANEL = 768
CAP = 48
TOKENS = 1536


def draw_activations(key, part):
    column_key = jax.random.fold_in(key, 11)
    position = jnp.arange(D, dtype=jnp.float32) / jnp.float32(max(D - 1, 1))
    column_scale = jnp.power(jnp.float32(10.0), 0.5 * position)
    values = jnp.clip(jax.random.normal(column_key, (TOKENS, D), jnp.float32), -6.0, 6.0)
    return (values * column_scale[None, :]).astype(jnp.bfloat16)


def assign_block(key, own, number, rows, amount, top, most, lean):
    sequence = jax.random.permutation(key, amount)
    heavy_load, common = load_shares(amount, rows * top, most, lean, True), load_shares(amount, rows * top, most, lean, False)
    places = jnp.arange(amount)

    def named(tallies, offset_by):
        used = int((tallies > 0).sum())
        fixed = max(1, used // 4)
        passed = fixed + (places - fixed + offset_by * (used - fixed)) % max(1, amount - fixed)
        return jnp.zeros((amount,), jnp.int32).at[sequence[jnp.where(places < fixed, places, passed)]].set(jnp.asarray(tallies, jnp.int32))

    tallies = jnp.where(number % 4 == 0, named(heavy_load, number // 4), named(common, number - number // 4 - 1))
    mixed = jax.random.permutation(jax.random.fold_in(own, 3), amount)
    giver, receiver = mixed[0:amount // 2 * 2:2], mixed[1:amount // 2 * 2:2]
    room = jnp.minimum(tallies[giver] - 1, most - tallies[receiver]) // 2
    room = jnp.where((giver == sequence[0]) | (receiver == sequence[0]) | (tallies[receiver] == 0), 0, jnp.maximum(room, 0))
    passed = jax.random.randint(jax.random.fold_in(own, 4), (amount // 2,), 0, 1 << 20) % (room + 1)
    tallies = tallies.at[giver].add(-passed).at[receiver].add(passed)
    labels = jnp.searchsorted(jnp.cumsum(tallies), jnp.arange(rows * top), side="right").astype(jnp.int32)
    grid = labels.reshape(top, rows).T
    grid = grid[jax.random.permutation(jax.random.fold_in(own, 1), rows)]
    offset_by = jax.random.randint(jax.random.fold_in(own, 2), (rows, 1), 0, top)
    return jnp.take_along_axis(grid, (jnp.arange(top)[None, :] + offset_by) % top, axis=1)


def load_shares(count, total, limit, lean, full):
    loads = [(1 << 20) // math.isqrt(grade ** lean) + 1 for grade in range(1, count + 1)]
    largest = limit if full else min(limit, max(-(-total // count), total * loads[0] // sum(loads)))
    least = 1 if total - largest >= count - 1 else 0
    given, rest = [largest] + [least] * (count - 1), total - largest - least * (count - 1)
    while rest > 0:
        candidates = [i for i in range(1, count) if given[i] < largest] or [i for i in range(1, count) if given[i] < limit]
        pool, remaining = sum([loads[i] for i in candidates]), rest
        for i in candidates:
            extra = min(limit - given[i], max(1, remaining * loads[i] // pool), rest)
            given[i] = given[i] + extra
            rest = rest - extra
    return np.array(given)


def setup_inputs(seed: int = 0) -> dict:
    splits = jax.random.split(jax.random.key(seed), 3)
    activations = draw_activations(jax.random.fold_in(splits[2], 71), 0)
    expert_ids_keys = jax.random.split(jax.random.fold_in(splits[1], 1), TOKENS // TOK_DEV)
    expert_ids_turns = jax.random.permutation(jax.random.fold_in(splits[1], 3), TOKENS // TOK_DEV)
    expert_ids = jax.vmap(lambda own, number: assign_block(jax.random.fold_in(splits[1], 2), own, number, TOK_DEV, EXPERTS, TOP, CAP, 2))(expert_ids_keys, expert_ids_turns).reshape((TOKENS, TOP))
    return dict(activations=activations, expert_ids=expert_ids)


damp_fraction = 0.01

def factor_panels(hessian):
    row_index = jnp.arange(D, dtype=jnp.int32)
    factors = []
    for panel in range(2):
        panel_start = panel * PANEL
        panel_block = hessian[:, panel_start:panel_start + PANEL]
        for earlier in factors:
            panel_block = panel_block - jnp.dot(earlier, earlier[panel_start:panel_start + PANEL].T, precision=lax.Precision.HIGHEST)
        diagonal_factor = jnp.linalg.cholesky(panel_block[panel_start:panel_start + PANEL])
        panel_factor = jax.scipy.linalg.solve_triangular(diagonal_factor, panel_block.T, lower=True).T
        column_index = panel_start + jnp.arange(PANEL, dtype=jnp.int32)
        lower_mask = row_index[:, None] >= column_index[None, :]
        factors.append(jnp.where(lower_mask, panel_factor, jnp.float32(0.0)))
    return jnp.concatenate(factors, axis=1)

def reference(activations, expert_ids):
    features = activations.astype(jnp.float32)
    expert_iota = jnp.arange(EXPERTS, dtype=jnp.int32)
    routed = jnp.sum((expert_ids[:, :, None] == expert_iota[None, None, :]).astype(jnp.float32), axis=1)
    counts = jnp.sum(routed, axis=0)
    identity = jnp.eye(D, dtype=jnp.float32)

    def one_expert(inputs):
        token_weight, expert_count = inputs
        gram_sum = jnp.dot((features * token_weight[:, None]).T, features, precision=lax.Precision.HIGHEST)
        hessian = gram_sum * (2.0 / expert_count)
        damping = damp_fraction * jnp.trace(hessian) / D
        hessian = hessian + damping * identity
        return (hessian, factor_panels(hessian))
    hessian, panels = lax.map(one_expert, (routed.T, counts))
    return (hessian, panels)
```

```python
import jax
import jax.numpy as jnp
from jax import lax
from jax.experimental import pallas as pl
from jax.experimental.pallas import tpu as pltpu
from jax.sharding import PartitionSpec as P

PANEL = 768
PANELS = 2
BLOCK = 128
EXTRA = 128

damp_fraction = 0.01
HIGHEST = lax.Precision.HIGHEST


def contract_rows(a, b):
    return lax.dot_general(
        a, b, (((0,), (0,)), ((), ())), precision=HIGHEST, preferred_element_type=jnp.float32
    )


def block_inverse(block):
    steps = BLOCK // 8
    sublane = lax.broadcasted_iota(jnp.int32, (8, BLOCK), 0)
    lane = lax.broadcasted_iota(jnp.int32, (8, BLOCK), 1)
    left = [block[8 * t : 8 * t + 8] for t in range(steps)]
    right = [jnp.where(lane == sublane + 8 * t, 1.0, 0.0).astype(jnp.float32) for t in range(steps)]
    for s in range(steps):
        rows_a, rows_i = left[s], right[s]
        columns = [
            jnp.broadcast_to(rows_a[:, 8 * s + m : 8 * s + m + 1], (8, BLOCK)) for m in range(8)
        ]
        for k in range(8):
            inv = lax.rsqrt(jnp.broadcast_to(columns[k][k : k + 1], (8, BLOCK)))
            scaled = columns[k] * inv
            below = jnp.where(sublane > k, scaled, 0.0)
            for m in range(k + 1, 8):
                columns[m] = columns[m] - below * jnp.broadcast_to(scaled[m : m + 1], (8, BLOCK))
            row_a = jnp.broadcast_to(rows_a[k : k + 1], (8, BLOCK)) * inv
            row_i = jnp.broadcast_to(rows_i[k : k + 1], (8, BLOCK)) * inv
            rows_a = jnp.where(sublane == k, row_a, rows_a - below * row_a)
            rows_i = jnp.where(sublane == k, row_i, rows_i - below * row_i)
        left[s], right[s] = rows_a, rows_i
        if s < steps - 1:
            update = contract_rows(rows_a, jnp.concatenate([rows_a, rows_i], axis=1))
            for t in range(s + 1, steps):
                left[t] = left[t] - update[8 * t : 8 * t + 8, :BLOCK]
                right[t] = right[t] - update[8 * t : 8 * t + 8, BLOCK:]
    return jnp.concatenate(right, axis=0)


def inverse_kernel(a_ref, out_ref, w_ref):
    n = w_ref.shape[0]
    blocks = n // BLOCK
    width = n + BLOCK
    pltpu.sync_copy(a_ref, w_ref.at[:, pl.ds(0, n)])
    row = lax.broadcasted_iota(jnp.int32, (BLOCK, n), 0)
    column = lax.broadcasted_iota(jnp.int32, (BLOCK, n), 1)

    @pl.loop(0, blocks)
    def _(b):
        start = pl.multiple_of(b * BLOCK, BLOCK)
        w_ref[pl.ds(start, BLOCK), pl.ds(n, n)] = jnp.where(
            row + start == column, 1.0, 0.0
        ).astype(jnp.float32)

    @pl.loop(0, blocks)
    def _(b):
        start = pl.multiple_of(b * BLOCK, BLOCK)
        rows = pl.ds(start, BLOCK)
        inverse = block_inverse(w_ref[rows, rows])
        w_ref[rows, pl.ds(start, width)] = jnp.dot(
            inverse,
            w_ref[rows, pl.ds(start, width)],
            precision=HIGHEST,
            preferred_element_type=jnp.float32,
        )

        @pl.loop(b + 1, blocks)
        def _(i):
            below = pl.ds(pl.multiple_of(i * BLOCK, BLOCK), BLOCK)
            w_ref[below, pl.ds(start, width)] = w_ref[below, pl.ds(start, width)] - contract_rows(
                w_ref[rows, below], w_ref[rows, pl.ds(start, width)]
            )

    pltpu.sync_copy(w_ref.at[:, pl.ds(n, n)], out_ref)


def cholesky_inverse(matrix):
    n = matrix.shape[0]
    return pl.pallas_call(
        inverse_kernel,
        out_shape=jax.ShapeDtypeStruct((n, n), jnp.float32),
        in_specs=[pl.BlockSpec(memory_space=pl.ANY)],
        out_specs=pl.BlockSpec(memory_space=pl.ANY),
        scratch_shapes=[pltpu.VMEM((n, 2 * n), jnp.float32)],
        compiler_params=pltpu.CompilerParams(vmem_limit_bytes=48 * 1024 * 1024),
        cost_estimate=pl.CostEstimate(
            flops=24 * n * n * n, bytes_accessed=8 * n * n, transcendentals=0
        ),
        name="cholesky_inverse",
    )(matrix)


def local(activations, expert_ids):
    tile_count = lax.axis_size("tile")
    tokens, feature_width = activations.shape
    rows_device = feature_width // tile_count
    tile_index = lax.axis_index("tile")
    expert = lax.axis_index("expert")
    width = PANELS * PANEL
    axes = ("expert", "tile")

    features = activations.astype(jnp.float32)
    norm = jnp.sum(features * features, axis=1, keepdims=True)
    high = lax.reduce_precision(norm, 8, 7)
    middle = lax.reduce_precision(norm - high, 8, 7)
    low = norm - high - middle
    side = jnp.concatenate([expert_ids.astype(jnp.float32), high, middle, low], axis=1)
    side = jnp.pad(side, ((0, 0), (0, EXTRA - side.shape[1]))).astype(jnp.bfloat16)
    first = lax.all_gather(
        jnp.concatenate([activations[:, :width], side], axis=1), axes, axis=0, tiled=True
    )
    rest_own, first = lax.optimization_barrier((activations[:, width:], first))
    rest = lax.all_gather(rest_own, axes, axis=0, tiled=True)

    top = expert_ids.shape[1]
    sides = first[:, width:].astype(jnp.float32)
    panel_features = first[:, :width]
    mask = jnp.any(sides[:, :top] == expert.astype(jnp.float32), axis=1)
    count = jnp.sum(mask.astype(jnp.float32))
    scale = 2.0 / count
    norms = jnp.sum(sides[:, top : top + 3], axis=1)
    trace = jnp.sum(jnp.where(mask, norms, 0.0)) * scale
    damping = damp_fraction * trace / feature_width

    def masked(part):
        return jnp.where(mask[:, None], part, jnp.bfloat16(0))

    def gram(a, b):
        return jnp.einsum("tr,tc->rc", a, b, preferred_element_type=jnp.float32)

    leading = gram(masked(panel_features), panel_features) * scale
    position = jnp.arange(width, dtype=jnp.int32)
    leading = leading + jnp.where(position[:, None] == position[None, :], damping, 0.0)
    inverse = cholesky_inverse(leading)

    start = tile_index * rows_device
    in_first = start < width
    own = jnp.where(
        in_first,
        lax.dynamic_slice_in_dim(panel_features, jnp.where(in_first, start, 0), rows_device, 1),
        lax.dynamic_slice_in_dim(rest, jnp.where(in_first, 0, start - width), rows_device, 1),
    )
    own = masked(own)
    hessian = jnp.concatenate([gram(own, panel_features), gram(own, rest)], axis=1) * scale
    global_rows = start + jnp.arange(rows_device, dtype=jnp.int32)
    columns = jnp.arange(feature_width, dtype=jnp.int32)
    hessian = hessian + jnp.where(global_rows[:, None] == columns[None, :], damping, 0.0)
    panels = lax.dot_general(
        hessian[:, :width], inverse, (((1,), (1,)), ((), ())), precision=HIGHEST
    )
    panels = jnp.where(global_rows[:, None] >= position[None, :], panels, 0.0)
    return (hessian[None], panels[None])


def solution(mesh):
    placed = (P(("expert", "tile"), None), P(("expert", "tile"), None))
    return jax.shard_map(
        local,
        mesh=mesh,
        in_specs=placed,
        out_specs=(P("expert", "tile", None), P("expert", "tile", None)),
        check_vma=False,
    )
```

```python
import jax
import jax.numpy as jnp
from jax import lax
from jax.experimental import pallas as pl
from jax.experimental.pallas import tpu as pltpu
from jax.sharding import PartitionSpec as P

PANEL = 768
PANELS = 2
BLOCK = 128
EXTRA = 128

damp_fraction = 0.01
HIGHEST = lax.Precision.HIGHEST


def contract_rows(a, b):
    return lax.dot_general(
        a, b, (((0,), (0,)), ((), ())), precision=HIGHEST, preferred_element_type=jnp.float32
    )


def block_inverse(block):
    steps = BLOCK // 8
    sublane = lax.broadcasted_iota(jnp.int32, (8, BLOCK), 0)
    lane = lax.broadcasted_iota(jnp.int32, (8, BLOCK), 1)
    left = [block[8 * t : 8 * t + 8] for t in range(steps)]
    right = [jnp.where(lane == sublane + 8 * t, 1.0, 0.0).astype(jnp.float32) for t in range(steps)]

    def spread(tile, s):
        return [jnp.broadcast_to(tile[:, 8 * s + m : 8 * s + m + 1], (8, BLOCK)) for m in range(8)]

    def row_of(tile, k):
        return jnp.broadcast_to(tile[k : k + 1], (8, BLOCK))

    for s in range(steps):
        rows_a, rows_i = left[s], right[s]
        columns = spread(rows_a, s)
        ahead = s + 1 < steps
        if ahead:
            next_a, next_i = left[s + 1], right[s + 1]
            next_columns = spread(next_a, s)
        for k in range(8):
            inv = lax.rsqrt(row_of(columns[k], k))
            square = inv * inv
            entries = [row_of(columns[k], m) if m > k else None for m in range(8)]
            below = jnp.where(sublane > k, columns[k], 0.0)
            for m in range(k + 1, 8):
                columns[m] = columns[m] - (below * entries[m]) * square
            row_a = row_of(rows_a, k) * inv
            row_i = row_of(rows_i, k) * inv
            factor = below * inv
            rows_a = jnp.where(sublane == k, row_a, rows_a - factor * row_a)
            rows_i = jnp.where(sublane == k, row_i, rows_i - factor * row_i)
            if ahead:
                factor = next_columns[k] * inv
                for m in range(k + 1, 8):
                    next_columns[m] = next_columns[m] - factor * (entries[m] * inv)
                next_a = next_a - factor * row_a
                next_i = next_i - factor * row_i
        left[s], right[s] = rows_a, rows_i
        if ahead:
            left[s + 1], right[s + 1] = next_a, next_i
        if s + 2 < steps:
            update = contract_rows(rows_a, jnp.concatenate([rows_a, rows_i], axis=1))
            for t in range(s + 2, steps):
                left[t] = left[t] - update[8 * t : 8 * t + 8, :BLOCK]
                right[t] = right[t] - update[8 * t : 8 * t + 8, BLOCK:]
    return jnp.concatenate(right, axis=0)


def three_terms(value):
    high = value.astype(jnp.bfloat16)
    rest = value - high.astype(jnp.float32)
    middle = rest.astype(jnp.bfloat16)
    low = (rest - middle.astype(jnp.float32)).astype(jnp.bfloat16)
    return high, middle, low


def stacked_left(value):
    h, m, l = three_terms(value)
    return jnp.concatenate([h, h, m, m, h, l], axis=1)


def inverse_kernel(a_ref, out_ref, w_ref, terms_ref):
    n = w_ref.shape[0]
    blocks = n // BLOCK
    width = n + BLOCK
    pltpu.sync_copy(a_ref, w_ref.at[:, pl.ds(0, n)])
    row = lax.broadcasted_iota(jnp.int32, (BLOCK, n), 0)
    column = lax.broadcasted_iota(jnp.int32, (BLOCK, n), 1)

    @pl.loop(0, blocks)
    def _(b):
        start = pl.multiple_of(b * BLOCK, BLOCK)
        w_ref[pl.ds(start, BLOCK), pl.ds(n, n)] = jnp.where(
            row + start == column, 1.0, 0.0
        ).astype(jnp.float32)

    def store_terms(value):
        h, m, l = three_terms(value)
        for place, term in enumerate((h, m, h, m, l, h)):
            terms_ref[pl.ds(place * BLOCK, BLOCK), :] = term

    @pl.loop(0, blocks)
    def _(b):
        start = pl.multiple_of(b * BLOCK, BLOCK)
        rows = pl.ds(start, BLOCK)
        window = pl.ds(start, width)
        inverse = block_inverse(w_ref[rows, rows])
        store_terms(w_ref[rows, window])
        scaled = jnp.dot(
            stacked_left(inverse), terms_ref[...], preferred_element_type=jnp.float32
        )
        w_ref[rows, window] = scaled
        store_terms(scaled)

        @pl.loop(b + 1, blocks)
        def _(i):
            below = pl.ds(pl.multiple_of(i * BLOCK, BLOCK), BLOCK)
            w_ref[below, window] = w_ref[below, window] - jnp.dot(
                stacked_left(w_ref[rows, below].T),
                terms_ref[...],
                preferred_element_type=jnp.float32,
            )

    pltpu.sync_copy(w_ref.at[:, pl.ds(n, n)], out_ref)


def cholesky_inverse(matrix):
    n = matrix.shape[0]
    return pl.pallas_call(
        inverse_kernel,
        out_shape=jax.ShapeDtypeStruct((n, n), jnp.float32),
        in_specs=[pl.BlockSpec(memory_space=pl.ANY)],
        out_specs=pl.BlockSpec(memory_space=pl.ANY),
        scratch_shapes=[
            pltpu.VMEM((n, 2 * n), jnp.float32),
            pltpu.VMEM((6 * BLOCK, n + BLOCK), jnp.bfloat16),
        ],
        compiler_params=pltpu.CompilerParams(vmem_limit_bytes=48 * 1024 * 1024),
        cost_estimate=pl.CostEstimate(
            flops=24 * n * n * n, bytes_accessed=8 * n * n, transcendentals=0
        ),
        name="cholesky_inverse",
    )(matrix)


def hessian_kernel(lead, numbers_ref, own_ref, first_ref, rest_ref, out_ref):
    step = pl.program_id(0)
    rows, columns = out_ref.shape
    scale, damping, start = numbers_ref[0], numbers_ref[1], numbers_ref[2]
    row = lax.broadcasted_iota(jnp.int32, (rows, columns), 0) + start.astype(jnp.int32)
    column = lax.broadcasted_iota(jnp.int32, (rows, columns), 1) + step * columns

    def finish(part_ref):
        total = jnp.dot(own_ref[...], part_ref[...], preferred_element_type=jnp.float32)
        out_ref[...] = total * scale + jnp.where(row == column, damping, 0.0)

    @pl.when(step < lead)
    def _():
        finish(first_ref)

    @pl.when(step >= lead)
    def _():
        finish(rest_ref)


def hessian_rows(numbers, own, first, rest, width):
    rows, tokens = own.shape
    block = 512
    lead = width // block
    steps = lead + rest.shape[1] // block
    return pl.pallas_call(
        lambda *refs: hessian_kernel(lead, *refs),
        grid=(steps,),
        out_shape=jax.ShapeDtypeStruct((rows, steps * block), jnp.float32),
        in_specs=[
            pl.BlockSpec(memory_space=pltpu.SMEM),
            pl.BlockSpec((rows, tokens), lambda j: (0, 0)),
            pl.BlockSpec((tokens, block), lambda j: (0, jnp.minimum(j, lead - 1))),
            pl.BlockSpec((tokens, block), lambda j: (0, jnp.maximum(j - lead, 0))),
        ],
        out_specs=pl.BlockSpec((rows, block), lambda j: (0, j)),
        compiler_params=pltpu.CompilerParams(vmem_limit_bytes=56 * 1024 * 1024),
        cost_estimate=pl.CostEstimate(
            flops=2 * rows * tokens * steps * block,
            bytes_accessed=4 * rows * steps * block + 2 * tokens * steps * block,
            transcendentals=0,
        ),
        name="hessian_rows",
    )(numbers, own, first, rest)


def local(activations, expert_ids):
    tile_count = lax.axis_size("tile")
    tokens, feature_width = activations.shape
    rows_device = feature_width // tile_count
    tile_index = lax.axis_index("tile")
    expert = lax.axis_index("expert")
    width = PANELS * PANEL
    axes = ("expert", "tile")

    features = activations.astype(jnp.float32)
    norm = jnp.sum(features * features, axis=1, keepdims=True)
    high = lax.reduce_precision(norm, 8, 7)
    middle = lax.reduce_precision(norm - high, 8, 7)
    low = norm - high - middle
    side = jnp.concatenate([expert_ids.astype(jnp.float32), high, middle, low], axis=1)
    side = jnp.pad(side, ((0, 0), (0, EXTRA - side.shape[1]))).astype(jnp.bfloat16)
    first = jnp.concatenate([activations[:, :width], side], axis=1)
    for axis in ("tile", "expert"):
        first = lax.all_gather(first, axis, axis=0, tiled=True)
    rest_own, first = lax.optimization_barrier((activations[:, width:], first))
    rest = lax.all_gather(rest_own, axes, axis=0, tiled=True)

    top = expert_ids.shape[1]
    sides = first[:, width:].astype(jnp.float32)
    panel_features = first[:, :width]
    mask = jnp.any(sides[:, :top] == expert.astype(jnp.float32), axis=1)
    count = jnp.sum(mask.astype(jnp.float32))
    scale = 2.0 / count
    norms = jnp.sum(sides[:, top : top + 3], axis=1)
    trace = jnp.sum(jnp.where(mask, norms, 0.0)) * scale
    damping = damp_fraction * trace / feature_width

    def masked(part):
        return jnp.where(mask[:, None], part, jnp.bfloat16(0))

    def gram(a, b):
        return jnp.einsum("tr,tc->rc", a, b, preferred_element_type=jnp.float32)

    leading = gram(masked(panel_features), panel_features) * scale
    position = jnp.arange(width, dtype=jnp.int32)
    leading = leading + jnp.where(position[:, None] == position[None, :], damping, 0.0)
    inverse = cholesky_inverse(leading)

    start = tile_index * rows_device
    in_first = start < width
    own = jnp.where(
        in_first,
        lax.dynamic_slice_in_dim(panel_features, jnp.where(in_first, start, 0), rows_device, 1),
        lax.dynamic_slice_in_dim(rest, jnp.where(in_first, 0, start - width), rows_device, 1),
    )
    numbers = jnp.stack([scale, damping, start.astype(jnp.float32)])
    hessian = hessian_rows(numbers, masked(own).T, first, rest, width)
    global_rows = start + jnp.arange(rows_device, dtype=jnp.int32)

    pieces = []
    for k in range(PANELS):
        end = (k + 1) * PANEL
        pieces.append(
            lax.dot_general(
                hessian[:, :end],
                inverse[k * PANEL : end, :end],
                (((1,), (1,)), ((), ())),
                precision=lax.Precision.HIGH,
                preferred_element_type=jnp.float32,
            )
        )
    panels = jnp.concatenate(pieces, axis=1)
    panels = jnp.where(global_rows[:, None] >= position[None, :], panels, 0.0)
    return (hessian[None], panels[None])


def solution(mesh):
    placed = (P(("expert", "tile"), None), P(("expert", "tile"), None))
    return jax.shard_map(
        local,
        mesh=mesh,
        in_specs=placed,
        out_specs=(P("expert", "tile", None), P("expert", "tile", None)),
        check_vma=False,
    )
```
